128 devices in a mesh: hst: 16 (over z, x_hi, core), head: 8 (over y, x_lo).
Axes of the slice: x: 4 (x_hi: 2, x_lo: 2; x = x_hi * 2 + x_lo), y: 4, z: 4, core: 2. Of those that a mesh axis runs over, the one named last changes fastest.
Arguments:
- query_rows: bfloat16 [16384, 8192], P(('hst', 'head')), may hold values from -9 to 9
- token_keys: bfloat16 [16384, 1024], P(('hst', 'head')), may hold values from -9 to 9
- token_values: bfloat16 [16384, 1024], P(('hst', 'head')), may hold values from -6 to 6
- offsets: int32 [16], P('hst'), may hold values from 0 to 4095
- anchor_owner: int32 [1], replicated, may hold values from 0 to 15
Outputs:
- attended: bfloat16 [16384, 8192], P(('hst', 'head'))
The draws below stay inside these ranges and needn't reach their ends.
Inputs may be any that keep to these rules, and one draw needn't show every extreme that they name: `offsets`: positions of block starts. `anchor_owner`: index of a block.
All inputs are finite; a program needn't handle non-finite values.
Results may differ from the reference program's by a relative error of at most 0.0095.
The reference program's roundings to bfloat16 on the way count: a program that leaves them out, or rounds other values in their place, can miss the bound.
Values may be sent and summed in bfloat16 or wider, within the bound.
A program may use at most 64 MiB of HBM per device.

```python
import jax
import jax.numpy as jnp
from jax import lax

QUERY_HEADS = 64
KEY_VALUE_HEADS = 8
HEAD_SIZE = 128
BLOCK_TOKENS = 1024
SEQUENCE_TOKENS = 16384
N_HST = 16


def draw_query_rows(key, part):
    key = jax.random.fold_in(key, 1)
    value_matrix = jnp.clip(jax.random.normal(key, (SEQUENCE_TOKENS, QUERY_HEADS, HEAD_SIZE), jnp.float32), -6.0, 6.0)
    return value_matrix.reshape(SEQUENCE_TOKENS, QUERY_HEADS * HEAD_SIZE).astype(jnp.bfloat16)


def draw_token_keys(key, part):
    key = jax.random.fold_in(key, 2)
    value_matrix = jnp.clip(jax.random.normal(key, (SEQUENCE_TOKENS, KEY_VALUE_HEADS, HEAD_SIZE), jnp.float32), -6.0, 6.0)
    return value_matrix.reshape(SEQUENCE_TOKENS, KEY_VALUE_HEADS * HEAD_SIZE).astype(jnp.bfloat16)


def plant(drawn, key, smallest, top_value):
    shape = drawn.shape
    place = [jax.random.randint(jax.random.fold_in(key, axis), (), 0, shape[axis]) for axis in range(len(shape))]
    drawn = drawn.at[tuple(place)].set(smallest)
    longest = shape.index(max(shape))
    place[longest] = (place[longest] + 1) % shape[longest]
    return drawn.at[tuple(place)].set(top_value)


def level_of(rng, dims, shards, least, largest):
    level = 1.0
    for dim, parts in shards:
        steps = jax.random.uniform(jax.random.fold_in(jax.random.fold_in(rng, 6), dim), (parts,), jnp.float32, least / len(shards), largest / len(shards))
        level = level * jnp.repeat(jnp.exp(steps), dims[dim] // parts).reshape((-1,) + (1,) * (len(dims) - 1 - dim))
    return level


def normal_values(own_key, shape, spread, bound, shards=(), kind=jnp.bfloat16):
    entries = jax.random.normal(own_key, shape, jnp.float32) * spread
    if len(shards) > 0:
        entries = level_of(own_key, shape, shards, -0.22, 0.18) * entries
    return jnp.clip(entries, min=-bound, max=bound).astype(kind)


def setup_inputs(seed: int = 0) -> dict:
    seeds = jax.random.split(jax.random.key(seed), 6)
    return {
        "query_rows": draw_query_rows(jax.random.fold_in(seeds[5], 71), 0),
        "token_keys": draw_token_keys(jax.random.fold_in(seeds[5], 71), 0),
        "token_values": normal_values(seeds[2], (SEQUENCE_TOKENS, KEY_VALUE_HEADS * HEAD_SIZE), 1.0, 6.0, ((0, 128),)),
        "offsets": plant(jax.random.randint(seeds[3], (N_HST,), 0, 4 * BLOCK_TOKENS), jax.random.fold_in(seeds[3], 1), 0, (4 * BLOCK_TOKENS) - 1).astype(jnp.int32),
        "anchor_owner": jax.random.randint(seeds[4], (1,), 0, N_HST).astype(jnp.int32),
    }


rope_theta = 500000.0


def apply_rotary(value_matrix, token_positions):
    width = value_matrix.shape[-1]
    half = width // 2
    exponents = jnp.arange(half, dtype=jnp.float32) * (2.0 / width)
    inverse = jnp.float32(rope_theta) ** (-exponents)
    angles = token_positions.astype(jnp.float32)[:, None] * inverse[None, :]
    doubled = jnp.concatenate([angles, angles], 1)
    cosine = jnp.cos(doubled)[:, None, :]
    sine = jnp.sin(doubled)[:, None, :]
    floats = value_matrix.astype(jnp.float32)
    turned = jnp.concatenate([-floats[..., half:], floats[..., :half]], -1)
    return (floats * cosine + turned * sine).astype(jnp.bfloat16)


def attend(queries, keys_local, values_local, keys_anchor, values_anchor, query_index, with_anchor):
    count = keys_local.shape[0]
    keys_all = jnp.concatenate([keys_anchor, keys_local], 0)
    values_all = jnp.concatenate([values_anchor, values_local], 0)
    scale = queries.shape[-1] ** -0.5
    scores = jnp.einsum("rgd,kd->grk", queries.astype(jnp.float32), keys_all.astype(jnp.float32)) * scale
    column = jnp.arange(2 * count, dtype=jnp.int32)
    allowed = jnp.where(column[None, :] < count, with_anchor, (column[None, :] - count) <= query_index[:, None])
    peak = jnp.max(jnp.where(allowed[None], scores, -jnp.inf), -1, keepdims=True)
    weights = jnp.where(allowed[None], jnp.exp(scores - peak), jnp.float32(0.0))
    total = jnp.sum(weights, -1, keepdims=True)
    mixed = jnp.einsum("grk,kd->grd", weights.astype(jnp.bfloat16).astype(jnp.float32), values_all.astype(jnp.float32)) / total
    return jnp.transpose(mixed, (1, 0, 2)).astype(jnp.bfloat16)


def reference(query_rows, token_keys, token_values, offsets, anchor_owner):
    query_group = QUERY_HEADS // KEY_VALUE_HEADS
    blocks_q = query_rows.reshape(N_HST, BLOCK_TOKENS, QUERY_HEADS, HEAD_SIZE)
    key_blocks = token_keys.reshape(N_HST, BLOCK_TOKENS, KEY_VALUE_HEADS, HEAD_SIZE)
    value_blocks = token_values.reshape(N_HST, BLOCK_TOKENS, KEY_VALUE_HEADS, HEAD_SIZE)
    within = jnp.arange(BLOCK_TOKENS, dtype=jnp.int32)
    chosen = anchor_owner[0].astype(jnp.int32)
    anchor_start = lax.dynamic_index_in_dim(offsets, chosen, 0, keepdims=False)
    anchor_keys = apply_rotary(lax.dynamic_index_in_dim(key_blocks, chosen, 0, keepdims=False), anchor_start + within)
    anchor_values = lax.dynamic_index_in_dim(value_blocks, chosen, 0, keepdims=False)

    def per_block(bundle):
        query_block, block_k, block_v, start, number = bundle
        token_positions = start + within
        spun_keys = apply_rotary(block_k, token_positions)
        spun_queries = apply_rotary(query_block, token_positions).reshape(BLOCK_TOKENS, KEY_VALUE_HEADS, query_group, HEAD_SIZE)
        with_anchor = number != chosen

        def per_head(pieces):
            head_q, head_k, head_v, anchor_k, anchor_v = pieces
            return attend(head_q, head_k, head_v, anchor_k, anchor_v, within, with_anchor)

        mixed = lax.map(per_head, (jnp.transpose(spun_queries, (1, 0, 2, 3)), jnp.transpose(spun_keys, (1, 0, 2)), jnp.transpose(block_v, (1, 0, 2)), jnp.transpose(anchor_keys, (1, 0, 2)), jnp.transpose(anchor_values, (1, 0, 2))))
        return jnp.transpose(mixed, (1, 0, 2, 3)).reshape(BLOCK_TOKENS, QUERY_HEADS * HEAD_SIZE)

    result = lax.map(per_block, (blocks_q, key_blocks, value_blocks, offsets, jnp.arange(N_HST, dtype=jnp.int32)))
    return result.reshape(N_HST * BLOCK_TOKENS, QUERY_HEADS * HEAD_SIZE)
```

```python
import functools

import jax
import jax.numpy as jnp
import numpy as np
from jax import lax
from jax.experimental import pallas as pl
from jax.experimental.pallas import tpu as pltpu
from jax.sharding import PartitionSpec as P

QUERY_HEADS = 64
KV = 8
D = 128
TOK = 128
ROPE_THETA = 500000.0
LOG2E_SCALE = float(D**-0.5 * np.log2(np.e))
F32 = jnp.float32
BF16 = jnp.bfloat16
MESH = pl.DeviceIdType.MESH
NT = (((1,), (1,)), ((), ()))
R = 512
MASKED = -1e30


def kernel(
    q_ref, k_ref, v_ref, inv_ref, off_ref, own_ref, out_ref,
    kvl, kva, cand, qs, s_scr, m_scr, bias, onesl, cos_scr, sin_scr,
    k1s, k1r, v1s, v1r, k2s, k2r, v3s, v3r, k3s, v2s,
    a0s, a0r, a2s, a2r, xs, xr, zs, zr, cxs, cxr,
):
    hst = lax.axis_index("hst")
    head = lax.axis_index("head")
    z, xh, c = hst // 4, (hst // 2) % 2, hst % 2
    y, xl = head // 2, head % 2
    h0 = 2 * z + xh

    def dev(zz, xxh, cc, yy, xxl):
        return ((zz * 2 + xxh) * 2 + cc, yy * 2 + xxl)

    partner = dev(z, xh, c, y, 1 - xl)
    across = dev(z, 1 - xh, c, y, 1 - xl)
    other = dev(z, xh, 1 - c, y, xl)

    bar = pltpu.get_barrier_semaphore()

    def greet_hst(r, _):
        pl.semaphore_signal(bar, inc=1, device_id=((hst + r) % 16, head), device_id_type=MESH)
        return 0

    def greet_head(r, _):
        pl.semaphore_signal(bar, inc=1, device_id=(hst, (head + r) % 8), device_id_type=MESH)
        return 0

    lax.fori_loop(1, 16, greet_hst, 0)
    lax.fori_loop(1, 8, greet_head, 0)
    pl.semaphore_signal(bar, inc=1, device_id=across, device_id_type=MESH)

    start = (off_ref[0] + head * TOK).astype(F32)
    pos = lax.broadcasted_iota(jnp.int32, (TOK, D), 0).astype(F32) + start
    lane = lax.broadcasted_iota(jnp.int32, (TOK, D), 1)
    ang = pos * inv_ref[...]
    cos_scr[...] = jnp.cos(ang)
    sine = jnp.sin(ang)
    sin_scr[...] = jnp.where(lane < D // 2, -sine, sine)

    def rotate(x):
        x = x.astype(F32)
        return (x * cos_scr[...] + pltpu.roll(x, D // 2, 1) * sin_scr[...]).astype(BF16)

    ro = pl.multiple_of(768 + xl * TOK, TOK)
    own_rows = pl.ds(ro, TOK)
    for h in range(KV):
        kvl[0, h, own_rows, :] = rotate(k_ref[:, h * D:(h + 1) * D])
        kvl[1, h, own_rows, :] = v_ref[:, h * D:(h + 1) * D]

    def rc(src, dst, ssem, rsem, device):
        return pltpu.make_async_remote_copy(
            src_ref=src, dst_ref=dst, send_sem=ssem, recv_sem=rsem, device_id=device, device_id_type=MESH
        )

    def offset(g):
        return g + (g // 2) * (1 - 2 * (g % 2))

    def pair(g):
        return 2 * ((z + offset(g)) % 4)

    def c_k1(g):
        ref = kvl.at[0, pl.ds(pair(g), 2), own_rows]
        return rc(ref, ref, k1s.at[g], k1r.at[g], partner)

    def v_rows(d):
        return own_rows if d == 0 else pl.ds(pl.multiple_of((3 - d) * 256 + xl * TOK, TOK), TOK)

    def v_rows_partner(d):
        return pl.ds(pl.multiple_of((3 - d) * 256 + (1 - xl) * TOK, TOK), TOK)

    def c_v1(g, d):
        return rc(kvl.at[1, pl.ds(pair(g), 2), own_rows], kvl.at[1, pl.ds(pair(g), 2), v_rows(d)],
                  v1s.at[g, d], v1r.at[g, d], dev(z, xh, c, (y + d) % 4, xl))

    def c_v2(g):
        return rc(kvl.at[1, pl.ds(pair(g), 2), v_rows(3)], kvl.at[1, pl.ds(pair(g), 2), v_rows(2)],
                  v2s.at[g], v1r.at[g, 2], dev(z, xh, c, (y + 3) % 4, xl))

    def c_v3(g, d):
        ref = kvl.at[1, pl.ds(pair(g), 2), v_rows(d)]
        return rc(ref, ref, v3s.at[g, d], v3r.at[g, d], partner)

    def c_k2(g, d):
        return rc(kvl.at[0, pl.ds(pair(g), 2), pl.ds(768, 256)], kvl.at[0, pl.ds(pair(g), 2), pl.ds((3 - d) * 256, 256)],
                  k2s.at[g, d], k2r.at[g, d], dev(z, xh, c, (y + d) % 4, xl))

    def c_k3(g):
        return rc(kvl.at[0, pl.ds(pair(g), 2), pl.ds(0, 256)], kvl.at[0, pl.ds(pair(g), 2), pl.ds(256, 256)],
                  k3s.at[g], k2r.at[g, 2], dev(z, xh, c, (y + 3) % 4, xl))

    ups = ((1, y < 3), (3, y == 0), (2, y == 1))

    def l1(g):
        c_k1(g).start()
        c_v3(g, 0).start()
        for d, cond in ups:
            @pl.when(cond)
            def _():
                c_v1(g, d).start()

    def l2(g):
        c_k1(g).wait_recv()
        for d, cond in ups:
            @pl.when(cond)
            def _():
                c_k2(g, d).start()
        for d in (1, 3, 2):
            @pl.when(y >= d)
            def _():
                c_v1(g, d).wait_recv()
                c_v3(g, d).start()
                if d == 3:
                    c_v2(g).start()

    def l2c(g):
        @pl.when(y == 3)
        def _():
            c_k2(g, 3).wait_recv()
            c_k3(g).start()

    def l3(g):
        c_v3(g, 0).wait_recv()
        for d in (1, 2):
            @pl.when(y >= d)
            def _():
                c_k2(g, d).wait_recv()
        for d in (1, 2, 3):
            @pl.when(y >= d)
            def _():
                c_v3(g, d).wait_recv()

    def l_sent(g):
        c_k1(g).wait_send()
        c_v3(g, 0).wait_send()
        for d, cond in ups:
            @pl.when(cond)
            def _():
                c_v1(g, d).wait_send()
                c_k2(g, d).wait_send()
        for d in (1, 2, 3):
            @pl.when(y >= d)
            def _():
                c_v3(g, d).wait_send()
                if d == 3:
                    c_v2(g).wait_send()
                    c_k3(g).wait_send()

    def c_a0(r):
        p = (hst + r) % 16
        return rc(kvl.at[p % 2, p // 2, own_rows], cand.at[hst], a0s.at[r], a0r.at[hst], (p, head))

    def c_a0_in(r):
        p = (hst + 16 - r) % 16
        return rc(cand.at[p], cand.at[p], a0s.at[r], a0r.at[p], (p, head))

    my_rows = pl.ds(pl.multiple_of(head * TOK, TOK), TOK)

    def c_a2(r):
        ref = kva.at[c, h0, my_rows]
        return rc(ref, ref, a2s.at[r], a2r.at[head], (hst, (head + r) % 8))

    def c_a2_in(r):
        s = (head + 8 - r) % 8
        ref = kva.at[c, h0, pl.ds(pl.multiple_of(s * TOK, TOK), TOK)]
        return rc(ref, ref, a2s.at[r], a2r.at[s], (hst, s))

    def c_cx(slot, kind, h, n):
        ref = kva.at[kind, pl.ds(h, n)]
        return rc(ref, ref, cxs.at[slot], cxr.at[slot], other)

    def c_x(d, h):
        ref = kva.at[c, pl.ds(h, 1)]
        return rc(ref, ref, xs.at[d], xr.at[d], across)

    def c_z(sub, d, h):
        ref = kva.at[c, pl.ds(h, 1)]
        return rc(ref, ref, zs.at[sub, d], zr.at[sub, d], dev((z + d) % 4, xh, c, y, xl))

    h1 = 2 * z + (1 - xh)

    def zr_step(g):
        d = 4 - offset(g)
        hp = pair(g)
        c_z(0, d, hp + xh).wait_recv()

        @pl.when(c == 0)
        def _():
            c_z(1, d, hp + 1 - xh).wait_recv()
            c_cx(1 + g, c, hp, 2).start()

        @pl.when(c == 1)
        def _():
            c_x(d, hp + xh).start()

    def xr_step(g):
        d = 4 - offset(g)
        hp = pair(g)

        @pl.when(c == 1)
        def _():
            c_x(d, hp + 1 - xh).wait_recv()
            c_cx(1 + g, c, hp, 2).start()

    def cxr_step(g):
        c_cx(1 + g, 1 - c, pair(g), 2).wait_recv()

    penalty = jnp.where(own_ref[0] == hst, -MASKED, 0.0).astype(F32)

    def qk(h, half, b):
        q = qs[pl.ds(pl.multiple_of((h * 8 + half * 4) * TOK, R), R), :]
        mx = []
        for part, src in ((0, kva), (1, kvl)):
            m = None
            for t in range(4):
                s = lax.dot_general(q, src[0, h, t * 256:(t + 1) * 256, :], NT, preferred_element_type=F32)
                if part == 1 and t == 3:
                    s = (s.reshape(R // TOK, TOK, 256) + bias[...][None]).reshape(R, 256)
                lo = part * 1024 + t * 256
                s_scr[b, :, lo:lo + 256] = s
                for u in range(2):
                    w = s[:, u * 128:(u + 1) * 128]
                    m = w if m is None else jnp.maximum(m, w)
            mx.append(m)
        m = jnp.maximum(mx[0] - penalty, mx[1])
        m_scr[b] = jnp.broadcast_to(jnp.max(m, 1, keepdims=True), (R, D)) * LOG2E_SCALE

    def pv(h, half, b):
        os = []
        for part, src in ((0, kva), (1, kvl)):
            m = m_scr[b] + penalty if part == 0 else m_scr[b]
            p = jnp.concatenate(
                [jnp.exp2(s_scr[b, :, lo:lo + 128] * LOG2E_SCALE - m).astype(BF16)
                 for lo in range(part * 1024, part * 1024 + 1024, 128)], 1)
            ones = jnp.ones((1024, D), BF16) if part == 0 else onesl[...]
            w = jnp.concatenate([src[1, h], ones], 1)
            os.append(jnp.dot(p, w, preferred_element_type=F32))
        o = os[0] + os[1]
        o = (o[:, :D] / o[:, D:]).astype(BF16)
        for i in range(R // TOK):
            col = pl.multiple_of((h * 8 + half * 4 + i) * D, D)
            out_ref[:, pl.ds(col, D)] = o[i * TOK:(i + 1) * TOK]

    def rotate_queries(h, _):
        for i in range(8):
            col = pl.multiple_of((h * 8 + i) * D, D)
            qs[pl.ds(col, TOK), :] = rotate(q_ref[:, pl.ds(col, D)])
        return 0

    pl.semaphore_wait(bar, 23)

    def start_a0(r, _):
        c_a0(r).start()
        return 0

    lax.fori_loop(1, 16, start_a0, 0)
    l1(0)

    t_i = lax.broadcasted_iota(jnp.int32, (TOK, 256), 0)
    k_i = lax.broadcasted_iota(jnp.int32, (TOK, 256), 1)
    bias[...] = jnp.where(k_i <= t_i + xl * TOK, 0.0, MASKED).astype(F32)
    onesl[768:1024] = jnp.ones((256, D), BF16)
    for d in (1, 2, 3):
        rows = slice((3 - d) * 256, (4 - d) * 256)

        @pl.when(y >= d)
        def _():
            onesl[rows] = jnp.ones((256, D), BF16)

        @pl.when(y < d)
        def _():
            onesl[rows] = jnp.zeros((256, D), BF16)

            def fill(h, _):
                first = kvl[0, h, own_rows, :][0:1].astype(F32)
                kvl[0, h, rows] = jnp.broadcast_to(first, (256, D)).astype(BF16)
                kvl[1, h, rows] = jnp.zeros((256, D), BF16)
                return 0

            lax.fori_loop(0, KV, fill, 0)

    cand[hst] = kvl[c, h0, own_rows, :]
    lax.fori_loop(0, 4, rotate_queries, 0)

    def wait_a0(r, _):
        c_a0_in(r).wait_recv()
        return 0

    lax.fori_loop(1, 16, wait_a0, 0)
    kva[c, h0, my_rows, :] = cand[own_ref[0]]

    def start_a2(r, _):
        c_a2(r).start()
        return 0

    lax.fori_loop(1, 8, start_a2, 0)
    l2(0)
    l1(1)
    lax.fori_loop(4, 8, rotate_queries, 0)

    def wait_a2(r, _):
        c_a2_in(r).wait_recv()
        return 0

    lax.fori_loop(1, 8, wait_a2, 0)
    c_cx(0, c, h0, 1).start()
    c_x(0, h0).start()
    c_z(0, 1, h0).start()
    c_z(0, 3, h0).start()
    l2c(0)
    c_x(0, h1).wait_recv()
    c_cx(1, c, h1, 1).start()

    @pl.when(c == 0)
    def _():
        c_z(1, 1, h1).start()
        c_z(1, 3, h1).start()

    l3(0)
    c_cx(0, 1 - c, h0, 1).wait_recv()

    qk(h0, 0, 0)

    def group(g, _):
        ha = pair(g) + xh
        hb = pair(g) + 1 - xh
        more = g < 3

        @pl.when(more)
        def _():
            l2(g + 1)

        @pl.when(g < 2)
        def _():
            l1(g + 2)

        qk(ha, 1, 1)
        pv(ha, 0, 0)

        @pl.when(g == 0)
        def _():
            c_z(0, 2, h0).start()

            @pl.when(c == 0)
            def _():
                c_z(1, 2, h1).start()

            c_cx(1, 1 - c, h1, 1).wait_recv()

        @pl.when(more)
        def _():
            l2c(g + 1)
            zr_step(g + 1)

        qk(hb, 0, 0)
        pv(ha, 1, 1)

        @pl.when(more)
        def _():
            xr_step(g + 1)

        qk(hb, 1, 1)
        pv(hb, 0, 0)

        @pl.when(more)
        def _():
            l3(g + 1)
            cxr_step(g + 1)

        nxt = jnp.minimum(g + 1, 3)
        qk(pair(nxt) + xh, 0, 0)
        pv(hb, 1, 1)
        return 0

    lax.fori_loop(0, 4, group, 0)

    def sent(g, _):
        l_sent(g)
        return 0

    lax.fori_loop(0, 4, sent, 0)

    def sent_a0(r, _):
        c_a0(r).wait_send()
        return 0

    lax.fori_loop(1, 16, sent_a0, 0)

    def sent_a2(r, _):
        c_a2(r).wait_send()
        return 0

    lax.fori_loop(1, 8, sent_a2, 0)
    c_cx(0, c, h0, 1).wait_send()
    c_cx(1, c, h1, 1).wait_send()
    c_x(0, h0).wait_send()

    def sent_z(g, _):
        d = 4 - offset(g)
        c_cx(1 + g, c, pair(g), 2).wait_send()
        c_z(0, d, h0).wait_send()

        @pl.when(c == 0)
        def _():
            c_z(1, d, h1).wait_send()

        @pl.when(c == 1)
        def _():
            c_x(d, pair(g) + xh).wait_send()

        return 0

    lax.fori_loop(1, 4, sent_z, 0)


def local(query_rows, token_keys, token_values, offsets, anchor_owner):
    exponents = np.arange(D // 2, dtype=np.float32) * np.float32(2.0 / D)
    inverse = (np.float64(ROPE_THETA) ** (-exponents.astype(np.float64))).astype(np.float32)
    inv = jnp.asarray(np.concatenate([inverse, inverse])[None, :])
    vmem = pl.BlockSpec(memory_space=pltpu.VMEM)
    smem = pl.BlockSpec(memory_space=pltpu.SMEM)
    dma = pltpu.SemaphoreType.DMA
    return pl.pallas_call(
        kernel,
        out_shape=jax.ShapeDtypeStruct(query_rows.shape, BF16),
        in_specs=[vmem, vmem, vmem, vmem, smem, smem],
        out_specs=vmem,
        scratch_shapes=[
            pltpu.VMEM((2, KV, 1024, D), BF16),
            pltpu.VMEM((2, KV, 1024, D), BF16),
            pltpu.VMEM((16, TOK, D), BF16),
            pltpu.VMEM((QUERY_HEADS * TOK, D), BF16),
            pltpu.VMEM((2, R, 2048), F32),
            pltpu.VMEM((2, R, D), F32),
            pltpu.VMEM((TOK, 256), F32),
            pltpu.VMEM((1024, D), BF16),
            pltpu.VMEM((TOK, D), F32),
            pltpu.VMEM((TOK, D), F32),
            dma((4,)), dma((4,)), dma((4, 4)), dma((4, 4)), dma((4, 4)), dma((4, 4)),
            dma((4, 4)), dma((4, 4)), dma((4,)), dma((4,)),
            dma((16,)), dma((16,)), dma((8,)), dma((8,)), dma((4,)), dma((4,)),
            dma((2, 4)), dma((2, 4)), dma((5,)), dma((5,)),
        ],
        compiler_params=pltpu.CompilerParams(
            collective_id=0, has_side_effects=True, vmem_limit_bytes=60 * 2**20
        ),
        name="star_attention",
    )(query_rows, token_keys, token_values, inv, offsets, anchor_owner)


def solution(mesh):
    return jax.shard_map(
        local,
        mesh=mesh,
        in_specs=(
            P(("hst", "head"), None),
            P(("hst", "head"), None),
            P(("hst", "head"), None),
            P("hst"),
            P(),
        ),
        out_specs=P(("hst", "head"), None),
        check_vma=False,
    )
```

```python
import functools

import jax
import jax.numpy as jnp
import numpy as np
from jax import lax
from jax.experimental import pallas as pl
from jax.experimental.pallas import tpu as pltpu
from jax.sharding import PartitionSpec as P

QUERY_HEADS = 64
KV = 8
D = 128
TOK = 128
ROPE_THETA = 500000.0
LOG2E_SCALE = float(D**-0.5 * np.log2(np.e))
F32 = jnp.float32
BF16 = jnp.bfloat16
MESH = pl.DeviceIdType.MESH
NT = (((1,), (1,)), ((), ()))
R = 512
MASKED = -1e30


def kernel(
    q_ref, k_ref, v_ref, inv_ref, off_ref, own_ref, out_ref,
    q_in, out_scr, kvl, kva, cand2, chosen, cand8, qs, s_scr, m_scr, bias, onesl, cos_scr, sin_scr,
    q_sem, out_sem, k1s, k1r, v1s, v1r, k2s, k2r, v3s, v3r, k3s,
    ps, pr, a0s, a0r, a2s, a2r, a3s, a3r, cxs, cxr,
):
    hst = lax.axis_index("hst")
    head = lax.axis_index("head")
    z, xh, c = hst // 4, (hst // 2) % 2, hst % 2
    y, xl = head // 2, head % 2
    h0 = 2 * z + xh

    def wrap(i, n):
        return jnp.where(i >= n, i - n, i)

    def dev(zz, xxh, cc, yy, xxl):
        return ((zz * 2 + xxh) * 2 + cc, yy * 2 + xxl)

    partner = dev(z, xh, c, y, 1 - xl)
    other = dev(z, xh, 1 - c, y, xl)
    zs = [z] + [wrap(z + d, 4) for d in (1, 2, 3)]
    ys = [y] + [wrap(y + d, 4) for d in (1, 2, 3)]

    def flipped(bit, flip):
        return 1 - bit if flip else bit

    def along(dz, flip):
        return dev(zs[dz], flipped(xh, flip), c, y, flipped(xl, flip))

    def beside(dy, flip):
        return dev(z, xh, c, ys[dy], flipped(xl, flip))

    CHIPS = [(0, 1), (1, 0), (3, 0), (1, 1), (3, 1), (2, 0), (2, 1)]
    BLOCK = [(0, 1), (1, 0), (1, 1), (3, 0), (3, 1), (2, 0), (2, 1)]

    q_load = pltpu.make_async_copy(q_ref, q_in, q_sem)
    q_load.start()

    def store(h):
        cols = pl.ds(pl.multiple_of(h * 1024, 1024), 1024)
        return pltpu.make_async_copy(out_scr.at[:, cols], out_ref.at[:, cols], out_sem.at[h])

    bar = pltpu.get_barrier_semaphore()
    for device in [other] + [along(*e) for e in CHIPS] + [beside(*e) for e in BLOCK]:
        pl.semaphore_signal(bar, inc=1, device_id=device, device_id_type=MESH)

    start = (off_ref[0] + head * TOK).astype(F32)
    pos = lax.broadcasted_iota(jnp.int32, (TOK, D), 0).astype(F32) + start
    lane = lax.broadcasted_iota(jnp.int32, (TOK, D), 1)
    ang = pos * inv_ref[...]
    cos_scr[...] = jnp.cos(ang)
    sine = jnp.sin(ang)
    sin_scr[...] = jnp.where(lane < D // 2, -sine, sine)

    def rotate(x):
        x = x.astype(F32)
        return (x * cos_scr[...] + pltpu.roll(x, D // 2, 1) * sin_scr[...]).astype(BF16)

    for h in range(KV):
        kvl[0, h, 3, xl] = rotate(k_ref[:, h * D:(h + 1) * D])
        kvl[1, h, 3, xl] = v_ref[:, h * D:(h + 1) * D]

    def rc(src, dst, ssem, rsem, device):
        return pltpu.make_async_remote_copy(
            src_ref=src, dst_ref=dst, send_sem=ssem, recv_sem=rsem, device_id=device, device_id_type=MESH
        )

    ZOFF = [0, 1, 3, 2]

    def two(g):
        return pl.ds(2 * zs[ZOFF[g]], 2)

    def c_k1(g):
        ref = kvl.at[:, two(g), 3, xl]
        return rc(ref, ref, k1s.at[g], k1r.at[g], partner)

    def c_v1(g, d):
        return rc(kvl.at[1, two(g), 3, xl], kvl.at[1, two(g), 3 - d, xl], v1s.at[g, d], v1r.at[g, d], beside(d, 0))

    def c_k2(g, d):
        return rc(kvl.at[0, two(g), 3], kvl.at[0, two(g), 3 - d], k2s.at[g, d], k2r.at[g, d], beside(d, 0))

    def c_v3(g, n):
        ref = kvl.at[1, two(g), pl.ds(3 - n, n), xl]
        return rc(ref, ref, v3s.at[g], v3r.at[g], partner)

    def c_k3(g, n):
        return rc(kvl.at[0, two(g), 0 if n == 3 else 2], kvl.at[0, two(g), 1], k3s.at[g], k2r.at[g, 2],
                  beside(3 if n == 3 else 1, 0))

    def ups(f, direct):
        for d, cond in ((3, y == 0), (1, y <= 2), (2, y <= 1)):
            if d != 2 or direct:
                @pl.when(cond)
                def _():
                    f(d)

    def at_y(f, ns=(1, 2, 3)):
        for n in ns:
            @pl.when(y == n)
            def _():
                f(n)

    def l1(g):
        c_k1(g).start()
        ups(lambda d: c_v1(g, d).start(), True)

    def l2k(g):
        c_k1(g).wait_recv()
        ups(lambda d: c_k2(g, d).start(), False)

    def l2v(g):
        for d in (1, 2, 3):
            @pl.when(y >= d)
            def _():
                c_v1(g, d).wait_recv()

        at_y(lambda n: c_v3(g, n).start())

    def l2c(g):
        def on(n):
            c_k2(g, 3 if n == 3 else 1).wait_recv()
            c_k3(g, n).start()

        at_y(on, (2, 3))

    def l3(g):
        @pl.when((y == 1) | (y == 3))
        def _():
            c_k2(g, 1).wait_recv()

        @pl.when(y >= 2)
        def _():
            c_k2(g, 2).wait_recv()

        at_y(lambda n: c_v3(g, n).wait_recv())

    def l_sent(g):
        c_k1(g).wait_send()
        ups(lambda d: c_v1(g, d).wait_send(), True)
        ups(lambda d: c_k2(g, d).wait_send(), False)
        at_y(lambda n: c_v3(g, n).wait_send())
        at_y(lambda n: c_k3(g, n).wait_send(), (2, 3))

    def c_p():
        return rc(kvl.at[1 - c, :, 3, xl], cand2.at[c], ps, pr, other)

    def c_p_in():
        return rc(cand2.at[1 - c], cand2.at[1 - c], ps, pr, other)

    def chip_head(e):
        return 2 * zs[e[0]] + flipped(xh, e[1])

    def c_a0(r):
        return rc(chosen.at[chip_head(CHIPS[r])], cand8.at[h0], a0s.at[r], a0r.at[h0], along(*CHIPS[r]))

    def c_a0_in(r):
        h = chip_head(CHIPS[r])
        return rc(cand8.at[h], cand8.at[h], a0s.at[r], a0r.at[h], along(*CHIPS[r]))

    def c_a2(r):
        ref = kva.at[c, h0, head]
        return rc(ref, ref, a2s.at[r], a2r.at[head], beside(*BLOCK[r]))

    def c_a2_in(r):
        s = 2 * ys[BLOCK[r][0]] + flipped(xl, BLOCK[r][1])
        ref = kva.at[c, h0, s]
        return rc(ref, ref, a2s.at[r], a2r.at[s], beside(*BLOCK[r]))

    def head_of(n):
        return h0 if n == 0 else chip_head(CHIPS[n - 1])

    def c_cx(n, kind):
        ref = kva.at[kind, head_of(n)]
        return rc(ref, ref, cxs.at[n], cxr.at[n], other)

    def to(n):
        dz, flip = CHIPS[n - 1]
        return along((4 - dz) % 4, flip)

    def c_a3(n):
        ref = kva.at[c, h0]
        return rc(ref, ref, a3s.at[n], a3r.at[n], to(n))

    def c_a3_on(n, keys):
        if keys:
            ref = kva.at[c, head_of(1)]
            return rc(ref, ref, a3s.at[n], a3r.at[n], along((4 - CHIPS[n - 1][0]) % 4, 0))
        ref = kva.at[c, head_of({4: 2, 5: 3, 7: 6}[n])]
        return rc(ref, ref, a3s.at[n], a3r.at[n], along(0, 1))

    def c_a3_in(n):
        ref = kva.at[c, head_of(n)]
        return rc(ref, ref, a3s.at[n], a3r.at[n], along(*CHIPS[n - 1]))

    def a_on(kind, *ns):
        @pl.when(c == kind)
        def _():
            for n in ns:
                c_a3_on(n, kind == 0).start()

    def a_in(n):
        c_a3_in(n).wait_recv()
        c_cx(n, c).start()
        if n == 1:
            a_on(0, 4, 5, 7)
        elif n in (2, 3, 6):
            a_on(1, {2: 4, 3: 5, 6: 7}[n])

    def cx_in(n):
        c_cx(n, 1 - c).wait_recv()

    penalty = jnp.where(own_ref[0] == hst, -MASKED, 0.0).astype(F32)

    def keys(src, h, t):
        if src is kva:
            return kva[0, h, 2 * t:2 * t + 2].reshape(256, D)
        return kvl[0, h, t].reshape(256, D)

    def qk(h, half, b):
        q = qs[pl.ds(pl.multiple_of((h * 8 + half * 4) * TOK, R), R), :]
        mx = []
        for part, src in ((0, kva), (1, kvl)):
            m = None
            for t in range(4):
                s = lax.dot_general(q, keys(src, h, t), NT, preferred_element_type=F32)
                if part == 1 and t == 3:
                    s = (s.reshape(R // TOK, TOK, 256) + bias[...][None]).reshape(R, 256)
                lo = part * 1024 + t * 256
                s_scr[b, :, lo:lo + 256] = s
                for u in range(2):
                    w = s[:, u * 128:(u + 1) * 128]
                    m = w if m is None else jnp.maximum(m, w)
            mx.append(m)
        m = jnp.maximum(mx[0] - penalty, mx[1])
        m_scr[b] = jnp.broadcast_to(jnp.max(m, 1, keepdims=True), (R, D)) * LOG2E_SCALE

    def pv(h, half, b):
        os = []
        for part, src in ((0, kva), (1, kvl)):
            m = m_scr[b] + penalty if part == 0 else m_scr[b]
            p = jnp.concatenate(
                [jnp.exp2(s_scr[b, :, lo:lo + 128] * LOG2E_SCALE - m).astype(BF16)
                 for lo in range(part * 1024, part * 1024 + 1024, 128)], 1)
            ones = jnp.ones((1024, D), BF16) if part == 0 else onesl[...]
            w = jnp.concatenate([src[1, h].reshape(1024, D), ones], 1)
            os.append(jnp.dot(p, w, preferred_element_type=F32))
        o = os[0] + os[1]
        o = (o[:, :D] / o[:, D:]).astype(BF16)
        for i in range(R // TOK):
            col = pl.multiple_of((h * 8 + half * 4 + i) * D, D)
            out_scr[:, pl.ds(col, D)] = o[i * TOK:(i + 1) * TOK]

    def rotate_queries(h, _):
        for i in range(8):
            col = pl.multiple_of((h * 8 + i) * D, D)
            qs[pl.ds(col, TOK), :] = rotate(q_in[:, pl.ds(col, D)])
        return 0

    pl.semaphore_wait(bar, 15)
    c_p().start()
    l1(0)
    l1(1)

    t_i = lax.broadcasted_iota(jnp.int32, (TOK, 256), 0)
    k_i = lax.broadcasted_iota(jnp.int32, (TOK, 256), 1)
    bias[...] = jnp.where(k_i <= t_i + xl * TOK, 0.0, MASKED).astype(F32)
    onesl[768:1024] = jnp.ones((256, D), BF16)
    cand2[c] = kvl[c, :, 3, xl]
    for d in (1, 2, 3):
        rows = slice((3 - d) * 256, (4 - d) * 256)

        @pl.when(y >= d)
        def _():
            onesl[rows] = jnp.ones((256, D), BF16)

        @pl.when(y < d)
        def _():
            onesl[rows] = jnp.zeros((256, D), BF16)

            def fill(h, _):
                first = kvl[0, h, 3, xl][0:1].astype(F32)
                kvl[0, h, 3 - d] = jnp.broadcast_to(first[None], (2, TOK, D)).astype(BF16)
                kvl[1, h, 3 - d] = jnp.zeros((2, TOK, D), BF16)
                return 0

            lax.fori_loop(0, KV, fill, 0)

    c_p_in().wait_recv()
    chosen[...] = cand2[own_ref[0] % 2]
    for r in range(7):
        c_a0(r).start()
    cand8[h0] = chosen[h0]
    q_load.wait()
    lax.fori_loop(0, 4, rotate_queries, 0)
    l2k(0)
    l2v(0)
    for r in range(7):
        c_a0_in(r).wait_recv()
    kva[c, h0, head] = cand8[own_ref[0] // 2]
    for r in range(7):
        c_a2(r).start()
    lax.fori_loop(4, 8, rotate_queries, 0)
    l2c(0)
    for r in range(7):
        c_a2_in(r).wait_recv()
    c_cx(0, c).start()
    for n in (1, 2, 3, 6):
        c_a3(n).start()
    l2k(1)
    l2v(1)
    l1(2)
    l1(3)
    l3(0)
    cx_in(0)

    qk(head_of(0), 0, 0)

    POLLS = {
        (0, 0): lambda: l2c(1),
        (0, 1): lambda: (l2k(2), l2v(2), a_in(1), a_in(2), a_in(3), cx_in(1)),
        (0, 2): lambda: (l2k(3), l2c(2), l3(1)),
        (0, 3): lambda: (l2v(3), cx_in(2)),
        (1, 0): lambda: l2c(3),
        (1, 1): lambda: (l3(2), cx_in(3)),
        (1, 2): lambda: (a_in(4), a_in(5), a_in(6)),
        (1, 3): lambda: cx_in(4),
        (2, 1): lambda: (cx_in(5), a_in(7)),
        (2, 2): lambda: l3(3),
        (2, 3): lambda: cx_in(6),
        (3, 1): lambda: cx_in(7),
    }

    def two_heads(it, _):
        def poll(j):
            for (i, jj), f in POLLS.items():
                if jj == j:
                    @pl.when(it == i)
                    def _():
                        f()

        def by_it(values):
            out = values[3]
            for i in (2, 1, 0):
                out = jnp.where(it == i, values[i], out)
            return out

        ha = by_it([head_of(n) for n in (0, 2, 4, 6)])
        hb = by_it([head_of(n) for n in (1, 3, 5, 7)])
        hn = by_it([head_of(n) for n in (2, 4, 6, 7)])

        poll(0)
        qk(ha, 1, 1)
        pv(ha, 0, 0)
        poll(1)
        qk(hb, 0, 0)
        pv(ha, 1, 1)
        store(ha).start()
        poll(2)
        qk(hb, 1, 1)
        pv(hb, 0, 0)
        poll(3)
        qk(hn, 0, 0)
        pv(hb, 1, 1)
        store(hb).start()
        return 0

    lax.fori_loop(0, 4, two_heads, 0)

    for g in range(4):
        l_sent(g)
    c_p().wait_send()
    for r in range(7):
        c_a0(r).wait_send()
        c_a2(r).wait_send()
        c_a3(r + 1).wait_send()
    for n in range(KV):
        c_cx(n, c).wait_send()
        store(n).wait()


def local(query_rows, token_keys, token_values, offsets, anchor_owner):
    exponents = np.arange(D // 2, dtype=np.float32) * np.float32(2.0 / D)
    inverse = (np.float64(ROPE_THETA) ** (-exponents.astype(np.float64))).astype(np.float32)
    inv = jnp.asarray(np.concatenate([inverse, inverse])[None, :])
    hbm = pl.BlockSpec(memory_space=pl.ANY)
    vmem = pl.BlockSpec(memory_space=pltpu.VMEM)
    smem = pl.BlockSpec(memory_space=pltpu.SMEM)
    dma = pltpu.SemaphoreType.DMA
    return pl.pallas_call(
        kernel,
        out_shape=jax.ShapeDtypeStruct(query_rows.shape, BF16),
        in_specs=[hbm, vmem, vmem, vmem, smem, smem],
        out_specs=hbm,
        scratch_shapes=[
            pltpu.VMEM((TOK, QUERY_HEADS * D), BF16),
            pltpu.VMEM((TOK, QUERY_HEADS * D), BF16),
            pltpu.VMEM((2, KV, 4, 2, TOK, D), BF16),
            pltpu.VMEM((2, KV, 8, TOK, D), BF16),
            pltpu.VMEM((2, KV, TOK, D), BF16),
            pltpu.VMEM((KV, TOK, D), BF16),
            pltpu.VMEM((KV, TOK, D), BF16),
            pltpu.VMEM((QUERY_HEADS * TOK, D), BF16),
            pltpu.VMEM((2, R, 2048), F32),
            pltpu.VMEM((2, R, D), F32),
            pltpu.VMEM((TOK, 256), F32),
            pltpu.VMEM((1024, D), BF16),
            pltpu.VMEM((TOK, D), F32),
            pltpu.VMEM((TOK, D), F32),
            dma, dma((8,)), dma((4,)), dma((4,)), dma((4, 4)), dma((4, 4)), dma((4, 4)), dma((4, 4)),
            dma((4,)), dma((4,)), dma((4,)), dma, dma, dma((8,)), dma((8,)), dma((8,)), dma((8,)),
            dma((8,)), dma((8,)), dma((8,)), dma((8,)),
        ],
        compiler_params=pltpu.CompilerParams(
            collective_id=0, has_side_effects=True, vmem_limit_bytes=60 * 2**20
        ),
        name="star_attention",
    )(query_rows, token_keys, token_values, inv, offsets, anchor_owner)


def solution(mesh):
    return jax.shard_map(
        local,
        mesh=mesh,
        in_specs=(
            P(("hst", "head"), None),
            P(("hst", "head"), None),
            P(("hst", "head"), None),
            P("hst"),
            P(),
        ),
        out_specs=P(("hst", "head"), None),
        check_vma=False,
    )
```

```python
import functools

import jax
import jax.numpy as jnp
import numpy as np
from jax import lax
from jax.experimental import pallas as pl
from jax.experimental.pallas import tpu as pltpu
from jax.sharding import PartitionSpec as P

QUERY_HEADS = 64
KV = 8
D = 128
TOK = 128
ROPE_THETA = 500000.0
LOG2E_SCALE = float(D**-0.5 * np.log2(np.e))
F32 = jnp.float32
BF16 = jnp.bfloat16
MESH = pl.DeviceIdType.MESH
NT = (((1,), (1,)), ((), ()))
R = 512
MASKED = -1e30


def kernel(
    q_ref, k_ref, v_ref, inv_ref, off_ref, own_ref, out_ref,
    q_in, kvl, kva, cand2, chosen, cand8, qs, s_scr, m_scr, bias, onesl, cos_scr, sin_scr,
    q_sem, k1s, k1r, v1s, v1r, k2s, k2r, v3s, v3r, k3s,
    ps, pr, a0s, a0r, a2s, a2r, a3s, a3r, cxs, cxr,
):
    hst = lax.axis_index("hst")
    head = lax.axis_index("head")
    z, xh, c = hst // 4, (hst // 2) % 2, hst % 2
    y, xl = head // 2, head % 2
    h0 = 2 * z + xh

    def wrap(i, n):
        return jnp.where(i >= n, i - n, i)

    def dev(zz, xxh, cc, yy, xxl):
        return ((zz * 2 + xxh) * 2 + cc, yy * 2 + xxl)

    partner = dev(z, xh, c, y, 1 - xl)
    other = dev(z, xh, 1 - c, y, xl)
    zs = [z] + [wrap(z + d, 4) for d in (1, 2, 3)]
    ys = [y] + [wrap(y + d, 4) for d in (1, 2, 3)]

    def flipped(bit, flip):
        return 1 - bit if flip else bit

    def along(dz, flip):
        return dev(zs[dz], flipped(xh, flip), c, y, flipped(xl, flip))

    def beside(dy, flip):
        return dev(z, xh, c, ys[dy], flipped(xl, flip))

    CHIPS = [(0, 1), (1, 0), (3, 0), (1, 1), (3, 1), (2, 0), (2, 1)]
    BLOCK = [(0, 1), (1, 0), (1, 1), (3, 0), (3, 1), (2, 0), (2, 1)]

    q_load = pltpu.make_async_copy(q_ref, q_in, q_sem)
    q_load.start()

    bar = pltpu.get_barrier_semaphore()
    for device in [other] + [along(*e) for e in CHIPS] + [beside(*e) for e in BLOCK]:
        pl.semaphore_signal(bar, inc=1, device_id=device, device_id_type=MESH)

    start = (off_ref[0] + head * TOK).astype(F32)
    pos = lax.broadcasted_iota(jnp.int32, (TOK, D), 0).astype(F32) + start
    lane = lax.broadcasted_iota(jnp.int32, (TOK, D), 1)
    ang = pos * inv_ref[...]
    cos_scr[...] = jnp.cos(ang)
    sine = jnp.sin(ang)
    sin_scr[...] = jnp.where(lane < D // 2, -sine, sine)

    def rotate(x):
        x = x.astype(F32)
        return (x * cos_scr[...] + pltpu.roll(x, D // 2, 1) * sin_scr[...]).astype(BF16)

    for h in range(KV):
        kvl[0, h, 3, xl] = rotate(k_ref[:, h * D:(h + 1) * D])
        kvl[1, h, 3, xl] = v_ref[:, h * D:(h + 1) * D]

    def rc(src, dst, ssem, rsem, device):
        return pltpu.make_async_remote_copy(
            src_ref=src, dst_ref=dst, send_sem=ssem, recv_sem=rsem, device_id=device, device_id_type=MESH
        )

    ZOFF = [0, 1, 3, 2]

    def two(g):
        return pl.ds(2 * zs[ZOFF[g]], 2)

    def c_k1(g):
        ref = kvl.at[:, two(g), 3, xl]
        return rc(ref, ref, k1s.at[g], k1r.at[g], partner)

    def c_v1(g, d):
        return rc(kvl.at[1, two(g), 3, xl], kvl.at[1, two(g), 3 - d, xl], v1s.at[g, d], v1r.at[g, d], beside(d, 0))

    def c_k2(g, d):
        return rc(kvl.at[0, two(g), 3], kvl.at[0, two(g), 3 - d], k2s.at[g, d], k2r.at[g, d], beside(d, 0))

    def c_v3(g, n):
        ref = kvl.at[1, two(g), pl.ds(3 - n, n), xl]
        return rc(ref, ref, v3s.at[g], v3r.at[g], partner)

    def c_k3(g, n):
        return rc(kvl.at[0, two(g), 0 if n == 3 else 2], kvl.at[0, two(g), 1], k3s.at[g], k2r.at[g, 2],
                  beside(3 if n == 3 else 1, 0))

    def ups(f, direct):
        for d, cond in ((3, y == 0), (1, y <= 2), (2, y <= 1)):
            if d != 2 or direct:
                @pl.when(cond)
                def _():
                    f(d)

    def at_y(f, ns=(1, 2, 3)):
        for n in ns:
            @pl.when(y == n)
            def _():
                f(n)

    def l1(g):
        c_k1(g).start()
        ups(lambda d: c_v1(g, d).start(), True)

    def l2k(g):
        c_k1(g).wait_recv()
        ups(lambda d: c_k2(g, d).start(), False)

    def l2v(g):
        for d in (1, 2, 3):
            @pl.when(y >= d)
            def _():
                c_v1(g, d).wait_recv()

        at_y(lambda n: c_v3(g, n).start())

    def l2c(g):
        def on(n):
            c_k2(g, 3 if n == 3 else 1).wait_recv()
            c_k3(g, n).start()

        at_y(on, (2, 3))

    def l3(g):
        @pl.when((y == 1) | (y == 3))
        def _():
            c_k2(g, 1).wait_recv()

        @pl.when(y >= 2)
        def _():
            c_k2(g, 2).wait_recv()

        at_y(lambda n: c_v3(g, n).wait_recv())

    def l_sent(g):
        c_k1(g).wait_send()
        ups(lambda d: c_v1(g, d).wait_send(), True)
        ups(lambda d: c_k2(g, d).wait_send(), False)
        at_y(lambda n: c_v3(g, n).wait_send())
        at_y(lambda n: c_k3(g, n).wait_send(), (2, 3))

    def c_p():
        return rc(kvl.at[1 - c, :, 3, xl], cand2.at[c], ps, pr, other)

    def c_p_in():
        return rc(cand2.at[1 - c], cand2.at[1 - c], ps, pr, other)

    def chip_head(e):
        return 2 * zs[e[0]] + flipped(xh, e[1])

    def c_a0(r):
        return rc(chosen.at[chip_head(CHIPS[r])], cand8.at[h0], a0s.at[r], a0r.at[h0], along(*CHIPS[r]))

    def c_a0_in(r):
        h = chip_head(CHIPS[r])
        return rc(cand8.at[h], cand8.at[h], a0s.at[r], a0r.at[h], along(*CHIPS[r]))

    def c_a2(r):
        ref = kva.at[c, h0, head]
        return rc(ref, ref, a2s.at[r], a2r.at[head], beside(*BLOCK[r]))

    def c_a2_in(r):
        s = 2 * ys[BLOCK[r][0]] + flipped(xl, BLOCK[r][1])
        ref = kva.at[c, h0, s]
        return rc(ref, ref, a2s.at[r], a2r.at[s], beside(*BLOCK[r]))

    def head_of(n):
        return h0 if n == 0 else chip_head(CHIPS[n - 1])

    def c_cx(n, kind):
        ref = kva.at[kind, head_of(n)]
        return rc(ref, ref, cxs.at[n], cxr.at[n], other)

    def to(n):
        dz, flip = CHIPS[n - 1]
        return along((4 - dz) % 4, flip)

    def c_a3(n):
        ref = kva.at[c, h0]
        return rc(ref, ref, a3s.at[n], a3r.at[n], to(n))

    def c_a3_on(n, keys):
        if keys:
            ref = kva.at[c, head_of(1)]
            return rc(ref, ref, a3s.at[n], a3r.at[n], along((4 - CHIPS[n - 1][0]) % 4, 0))
        ref = kva.at[c, head_of({4: 2, 5: 3, 7: 6}[n])]
        return rc(ref, ref, a3s.at[n], a3r.at[n], along(0, 1))

    def c_a3_in(n):
        ref = kva.at[c, head_of(n)]
        return rc(ref, ref, a3s.at[n], a3r.at[n], along(*CHIPS[n - 1]))

    def a_on(kind, *ns):
        @pl.when(c == kind)
        def _():
            for n in ns:
                c_a3_on(n, kind == 0).start()

    def a_in(n):
        c_a3_in(n).wait_recv()
        c_cx(n, c).start()
        if n == 1:
            a_on(0, 4, 5, 7)
        elif n in (2, 3, 6):
            a_on(1, {2: 4, 3: 5, 6: 7}[n])

    def cx_in(n):
        c_cx(n, 1 - c).wait_recv()

    penalty = jnp.where(own_ref[0] == hst, -MASKED, 0.0).astype(F32)

    def keys(src, h, t):
        if src is kva:
            return kva[0, h, 2 * t:2 * t + 2].reshape(256, D)
        return kvl[0, h, t].reshape(256, D)

    def qk(h, half, b):
        q = qs[pl.ds(pl.multiple_of((h * 8 + half * 4) * TOK, R), R), :]
        mx = []
        for part, src in ((0, kva), (1, kvl)):
            m = None
            for t in range(4):
                s = lax.dot_general(q, keys(src, h, t), NT, preferred_element_type=F32)
                if part == 1 and t == 3:
                    s = (s.reshape(R // TOK, TOK, 256) + bias[...][None]).reshape(R, 256)
                lo = part * 1024 + t * 256
                s_scr[b, :, lo:lo + 256] = s
                for u in range(2):
                    w = s[:, u * 128:(u + 1) * 128]
                    m = w if m is None else jnp.maximum(m, w)
            mx.append(m)
        m = jnp.maximum(mx[0] - penalty, mx[1])
        m_scr[b] = jnp.broadcast_to(jnp.max(m, 1, keepdims=True), (R, D)) * LOG2E_SCALE

    def pv(h, half, b):
        os = []
        for part, src in ((0, kva), (1, kvl)):
            m = m_scr[b] + penalty if part == 0 else m_scr[b]
            p = jnp.concatenate(
                [jnp.exp2(s_scr[b, :, lo:lo + 128] * LOG2E_SCALE - m).astype(BF16)
                 for lo in range(part * 1024, part * 1024 + 1024, 128)], 1)
            ones = jnp.ones((1024, D), BF16) if part == 0 else onesl[...]
            w = jnp.concatenate([src[1, h].reshape(1024, D), ones], 1)
            os.append(jnp.dot(p, w, preferred_element_type=F32))
        o = os[0] + os[1]
        o = (o[:, :D] / o[:, D:]).astype(BF16)
        for i in range(R // TOK):
            col = pl.multiple_of((h * 8 + half * 4 + i) * D, D)
            out_ref[:, pl.ds(col, D)] = o[i * TOK:(i + 1) * TOK]

    def rotate_queries(h, _):
        for i in range(8):
            col = pl.multiple_of((h * 8 + i) * D, D)
            qs[pl.ds(col, TOK), :] = rotate(q_in[:, pl.ds(col, D)])
        return 0

    pl.semaphore_wait(bar, 15)
    c_p().start()
    l1(0)
    l1(1)

    t_i = lax.broadcasted_iota(jnp.int32, (TOK, 256), 0)
    k_i = lax.broadcasted_iota(jnp.int32, (TOK, 256), 1)
    bias[...] = jnp.where(k_i <= t_i + xl * TOK, 0.0, MASKED).astype(F32)
    onesl[768:1024] = jnp.ones((256, D), BF16)
    cand2[c] = kvl[c, :, 3, xl]
    for d in (1, 2, 3):
        rows = slice((3 - d) * 256, (4 - d) * 256)

        @pl.when(y >= d)
        def _():
            onesl[rows] = jnp.ones((256, D), BF16)

        @pl.when(y < d)
        def _():
            onesl[rows] = jnp.zeros((256, D), BF16)

            def fill(h, _):
                first = kvl[0, h, 3, xl][0:1].astype(F32)
                kvl[0, h, 3 - d] = jnp.broadcast_to(first[None], (2, TOK, D)).astype(BF16)
                kvl[1, h, 3 - d] = jnp.zeros((2, TOK, D), BF16)
                return 0

            lax.fori_loop(0, KV, fill, 0)

    c_p_in().wait_recv()
    chosen[...] = cand2[own_ref[0] % 2]
    for r in range(7):
        c_a0(r).start()
    cand8[h0] = chosen[h0]
    q_load.wait()
    lax.fori_loop(0, 4, rotate_queries, 0)
    l2k(0)
    l2v(0)
    for r in range(7):
        c_a0_in(r).wait_recv()
    kva[c, h0, head] = cand8[own_ref[0] // 2]
    for r in range(7):
        c_a2(r).start()
    lax.fori_loop(4, 8, rotate_queries, 0)
    l2k(1)
    l2v(1)
    l2c(0)
    for r in range(7):
        c_a2_in(r).wait_recv()
    c_cx(0, c).start()
    for n in (1, 2, 3, 6):
        c_a3(n).start()
    l1(2)
    l1(3)
    l3(0)
    cx_in(0)

    qk(head_of(0), 0, 0)

    POLLS = {
        (0, 0): lambda: (l2c(1),),
        (0, 1): lambda: (l2k(2), l2v(2), a_in(1), a_in(2), a_in(3), cx_in(1),),
        (0, 2): lambda: (l2k(3), l2c(2), l3(1),),
        (0, 3): lambda: (l2v(3), cx_in(2),),
        (1, 0): lambda: (l2c(3),),
        (1, 1): lambda: (l3(2), cx_in(3),),
        (1, 2): lambda: (a_in(4), a_in(5), a_in(6),),
        (1, 3): lambda: (cx_in(4),),
        (2, 1): lambda: (cx_in(5), a_in(7),),
        (2, 2): lambda: (l3(3),),
        (2, 3): lambda: (cx_in(6),),
        (3, 1): lambda: (cx_in(7),),
    }

    def two_heads(it, _):
        def poll(j):
            for (i, jj), f in POLLS.items():
                if jj == j:
                    @pl.when(it == i)
                    def _():
                        f()

        def by_it(values):
            out = values[3]
            for i in (2, 1, 0):
                out = jnp.where(it == i, values[i], out)
            return out

        ha = by_it([head_of(n) for n in (0, 2, 4, 6)])
        hb = by_it([head_of(n) for n in (1, 3, 5, 7)])
        hn = by_it([head_of(n) for n in (2, 4, 6, 7)])

        poll(0)
        qk(ha, 1, 1)
        pv(ha, 0, 0)
        poll(1)
        qk(hb, 0, 0)
        pv(ha, 1, 1)
        poll(2)
        qk(hb, 1, 1)
        pv(hb, 0, 0)
        poll(3)
        qk(hn, 0, 0)
        pv(hb, 1, 1)
        return 0

    lax.fori_loop(0, 4, two_heads, 0)

    for g in range(4):
        l_sent(g)
    c_p().wait_send()
    for r in range(7):
        c_a0(r).wait_send()
        c_a2(r).wait_send()
        c_a3(r + 1).wait_send()
    for n in range(KV):
        c_cx(n, c).wait_send()


def local(query_rows, token_keys, token_values, offsets, anchor_owner):
    exponents = np.arange(D // 2, dtype=np.float32) * np.float32(2.0 / D)
    inverse = (np.float64(ROPE_THETA) ** (-exponents.astype(np.float64))).astype(np.float32)
    inv = jnp.asarray(np.concatenate([inverse, inverse])[None, :])
    hbm = pl.BlockSpec(memory_space=pl.ANY)
    vmem = pl.BlockSpec(memory_space=pltpu.VMEM)
    smem = pl.BlockSpec(memory_space=pltpu.SMEM)
    dma = pltpu.SemaphoreType.DMA
    return pl.pallas_call(
        kernel,
        out_shape=pltpu.VMEM(query_rows.shape, BF16),
        in_specs=[hbm, vmem, vmem, vmem, smem, smem],
        out_specs=vmem,
        scratch_shapes=[
            pltpu.VMEM((TOK, QUERY_HEADS * D), BF16),
            pltpu.VMEM((2, KV, 4, 2, TOK, D), BF16),
            pltpu.VMEM((2, KV, 8, TOK, D), BF16),
            pltpu.VMEM((2, KV, TOK, D), BF16),
            pltpu.VMEM((KV, TOK, D), BF16),
            pltpu.VMEM((KV, TOK, D), BF16),
            pltpu.VMEM((QUERY_HEADS * TOK, D), BF16),
            pltpu.VMEM((2, R, 2048), F32),
            pltpu.VMEM((2, R, D), F32),
            pltpu.VMEM((TOK, 256), F32),
            pltpu.VMEM((1024, D), BF16),
            pltpu.VMEM((TOK, D), F32),
            pltpu.VMEM((TOK, D), F32),
            dma, dma((4,)), dma((4,)), dma((4, 4)), dma((4, 4)), dma((4, 4)), dma((4, 4)),
            dma((4,)), dma((4,)), dma((4,)), dma, dma, dma((8,)), dma((8,)), dma((8,)), dma((8,)),
            dma((8,)), dma((8,)), dma((8,)), dma((8,)),
        ],
        compiler_params=pltpu.CompilerParams(
            collective_id=0, has_side_effects=True, vmem_limit_bytes=60 * 2**20
        ),
        name="star_attention",
    )(query_rows, token_keys, token_values, inv, offsets, anchor_owner)


def solution(mesh):
    return jax.shard_map(
        local,
        mesh=mesh,
        in_specs=(
            P(("hst", "head"), None),
            P(("hst", "head"), None),
            P(("hst", "head"), None),
            P("hst"),
            P(),
        ),
        out_specs=P(("hst", "head"), None),
        check_vma=False,
    )
```

```python
import functools

import jax
import jax.numpy as jnp
import numpy as np
from jax import lax
from jax.experimental import pallas as pl
from jax.experimental.pallas import tpu as pltpu
from jax.sharding import PartitionSpec as P

QUERY_HEADS = 64
KV = 8
D = 128
TOK = 128
ROPE_THETA = 500000.0
LOG2E_SCALE = float(D**-0.5 * np.log2(np.e))
F32 = jnp.float32
BF16 = jnp.bfloat16
MESH = pl.DeviceIdType.MESH
NT = (((1,), (1,)), ((), ()))
R = 512
MASKED = -1e30


def kernel(
    q_ref, k_ref, v_ref, inv_ref, off_ref, own_ref, out_ref,
    q_in, kvl, kva, cand2, chosen, cand8, qs, s_scr, m_scr, bias, onesl, cos_scr, sin_scr,
    q_sem, k1s, k1r, v1s, v1r, k2s, k2r, v3s, v3r, k3s,
    ps, pr, a0s, a0r, a2s, a2r, a3s, a3r, cxs, cxr,
):
    hst = lax.axis_index("hst")
    head = lax.axis_index("head")
    z, xh, c = hst // 4, (hst // 2) % 2, hst % 2
    y, xl = head // 2, head % 2
    h0 = 2 * z + xh

    def wrap(i, n):
        return jnp.where(i >= n, i - n, i)

    def dev(zz, xxh, cc, yy, xxl):
        return ((zz * 2 + xxh) * 2 + cc, yy * 2 + xxl)

    partner = dev(z, xh, c, y, 1 - xl)
    other = dev(z, xh, 1 - c, y, xl)
    zs = [z] + [wrap(z + d, 4) for d in (1, 2, 3)]
    ys = [y] + [wrap(y + d, 4) for d in (1, 2, 3)]

    def flipped(bit, flip):
        return 1 - bit if flip else bit

    def along(dz, flip):
        return dev(zs[dz], flipped(xh, flip), c, y, flipped(xl, flip))

    def beside(dy, flip):
        return dev(z, xh, c, ys[dy], flipped(xl, flip))

    CHIPS = [(0, 1), (1, 0), (3, 0), (1, 1), (3, 1), (2, 0), (2, 1)]
    BLOCK = [(0, 1), (1, 0), (1, 1), (3, 0), (3, 1), (2, 0), (2, 1)]

    q_load = pltpu.make_async_copy(q_ref, q_in, q_sem)
    q_load.start()

    bar = pltpu.get_barrier_semaphore()
    for device in [other] + [along(*e) for e in CHIPS] + [beside(*e) for e in BLOCK]:
        pl.semaphore_signal(bar, inc=1, device_id=device, device_id_type=MESH)

    start = (off_ref[0] + head * TOK).astype(F32)
    pos = lax.broadcasted_iota(jnp.int32, (TOK, D), 0).astype(F32) + start
    lane = lax.broadcasted_iota(jnp.int32, (TOK, D), 1)
    ang = pos * inv_ref[...]
    cos_scr[...] = jnp.cos(ang)
    sine = jnp.sin(ang)
    sin_scr[...] = jnp.where(lane < D // 2, -sine, sine)

    def rotate(x):
        x = x.astype(F32)
        return (x * cos_scr[...] + pltpu.roll(x, D // 2, 1) * sin_scr[...]).astype(BF16)

    for h in range(KV):
        kvl[0, h, 3, xl] = rotate(k_ref[:, h * D:(h + 1) * D])
        kvl[1, h, 3, xl] = v_ref[:, h * D:(h + 1) * D]

    def rc(src, dst, ssem, rsem, device):
        return pltpu.make_async_remote_copy(
            src_ref=src, dst_ref=dst, send_sem=ssem, recv_sem=rsem, device_id=device, device_id_type=MESH
        )

    ZOFF = [0, 1, 3, 2]

    def two(g):
        return pl.ds(2 * zs[ZOFF[g]], 2)

    def c_k1(g):
        ref = kvl.at[:, two(g), 3, xl]
        return rc(ref, ref, k1s.at[g], k1r.at[g], partner)

    def c_v1(g, d):
        return rc(kvl.at[1, two(g), 3, xl], kvl.at[1, two(g), 3 - d, xl], v1s.at[g, d], v1r.at[g, d], beside(d, 0))

    def c_k2(g, d):
        return rc(kvl.at[0, two(g), 3], kvl.at[0, two(g), 3 - d], k2s.at[g, d], k2r.at[g, d], beside(d, 0))

    def c_v3(g, n):
        ref = kvl.at[1, two(g), pl.ds(3 - n, n), xl]
        return rc(ref, ref, v3s.at[g], v3r.at[g], partner)

    def c_k3(g, n):
        return rc(kvl.at[0, two(g), 0 if n == 3 else 2], kvl.at[0, two(g), 1], k3s.at[g], k2r.at[g, 2],
                  beside(3 if n == 3 else 1, 0))

    def ups(f, direct):
        for d, cond in ((3, y == 0), (1, y <= 2), (2, y <= 1)):
            if d != 2 or direct:
                @pl.when(cond)
                def _():
                    f(d)

    def at_y(f, ns=(1, 2, 3)):
        for n in ns:
            @pl.when(y == n)
            def _():
                f(n)

    def l1(g):
        c_k1(g).start()
        ups(lambda d: c_v1(g, d).start(), True)

    def l2k(g):
        c_k1(g).wait_recv()
        ups(lambda d: c_k2(g, d).start(), False)

    def l2v(g):
        for d in (1, 2, 3):
            @pl.when(y >= d)
            def _():
                c_v1(g, d).wait_recv()

        at_y(lambda n: c_v3(g, n).start())

    def l2c(g):
        def on(n):
            c_k2(g, 3 if n == 3 else 1).wait_recv()
            c_k3(g, n).start()

        at_y(on, (2, 3))

    def l3(g):
        @pl.when((y == 1) | (y == 3))
        def _():
            c_k2(g, 1).wait_recv()

        @pl.when(y >= 2)
        def _():
            c_k2(g, 2).wait_recv()

        at_y(lambda n: c_v3(g, n).wait_recv())

    def l_sent(g):
        c_k1(g).wait_send()
        ups(lambda d: c_v1(g, d).wait_send(), True)
        ups(lambda d: c_k2(g, d).wait_send(), False)
        at_y(lambda n: c_v3(g, n).wait_send())
        at_y(lambda n: c_k3(g, n).wait_send(), (2, 3))

    def c_p():
        return rc(kvl.at[1 - c, :, 3, xl], cand2.at[c], ps, pr, other)

    def c_p_in():
        return rc(cand2.at[1 - c], cand2.at[1 - c], ps, pr, other)

    def chip_head(e):
        return 2 * zs[e[0]] + flipped(xh, e[1])

    def c_a0(r):
        return rc(chosen.at[chip_head(CHIPS[r])], cand8.at[h0], a0s.at[r], a0r.at[h0], along(*CHIPS[r]))

    def c_a0_in(r):
        h = chip_head(CHIPS[r])
        return rc(cand8.at[h], cand8.at[h], a0s.at[r], a0r.at[h], along(*CHIPS[r]))

    def c_a2(r):
        ref = kva.at[c, h0, head]
        return rc(ref, ref, a2s.at[r], a2r.at[head], beside(*BLOCK[r]))

    def c_a2_in(r):
        s = 2 * ys[BLOCK[r][0]] + flipped(xl, BLOCK[r][1])
        ref = kva.at[c, h0, s]
        return rc(ref, ref, a2s.at[r], a2r.at[s], beside(*BLOCK[r]))

    def head_of(n):
        return h0 if n == 0 else chip_head(CHIPS[n - 1])

    def c_cx(n, kind):
        ref = kva.at[kind, head_of(n)]
        return rc(ref, ref, cxs.at[n], cxr.at[n], other)

    def to(n):
        dz, flip = CHIPS[n - 1]
        return along((4 - dz) % 4, flip)

    def c_a3(n):
        ref = kva.at[c, h0]
        return rc(ref, ref, a3s.at[n], a3r.at[n], to(n))

    def c_a3_on(n, keys):
        if keys:
            ref = kva.at[c, head_of(1)]
            return rc(ref, ref, a3s.at[n], a3r.at[n], along((4 - CHIPS[n - 1][0]) % 4, 0))
        ref = kva.at[c, head_of({4: 2, 5: 3, 7: 6}[n])]
        return rc(ref, ref, a3s.at[n], a3r.at[n], along(0, 1))

    def c_a3_in(n):
        ref = kva.at[c, head_of(n)]
        return rc(ref, ref, a3s.at[n], a3r.at[n], along(*CHIPS[n - 1]))

    def a_on(kind, *ns):
        @pl.when(c == kind)
        def _():
            for n in ns:
                c_a3_on(n, kind == 0).start()

    def a_in(n):
        c_a3_in(n).wait_recv()
        c_cx(n, c).start()
        if n == 1:
            a_on(0, 4, 5, 7)
        elif n in (2, 3, 6):
            a_on(1, {2: 4, 3: 5, 6: 7}[n])

    def cx_in(n):
        c_cx(n, 1 - c).wait_recv()

    penalty = jnp.where(own_ref[0] == hst, -MASKED, 0.0).astype(F32)

    def keys(src, h, t):
        if src is kva:
            return kva[0, h, 2 * t:2 * t + 2].reshape(256, D)
        return kvl[0, h, t].reshape(256, D)

    def scores(h, half, b, part, src):
        q = qs[pl.ds(pl.multiple_of((h * 8 + half * 4) * TOK, R), R), :]
        m = None
        for t in range(4):
            s = lax.dot_general(q, keys(src, h, t), NT, preferred_element_type=F32)
            if part == 1 and t == 3:
                s = (s.reshape(R // TOK, TOK, 256) + bias[...][None]).reshape(R, 256)
            lo = part * 1024 + t * 256
            s_scr[b, :, lo:lo + 256] = s
            for u in range(2):
                w = s[:, u * 128:(u + 1) * 128]
                m = w if m is None else jnp.maximum(m, w)
        return m

    def close(b, m_anchor, m_local):
        m = jnp.maximum(m_anchor - penalty, m_local)
        m_scr[b] = jnp.broadcast_to(jnp.max(m, 1, keepdims=True), (R, D)) * LOG2E_SCALE

    def qk(h, half, b):
        close(b, scores(h, half, b, 0, kva), scores(h, half, b, 1, kvl))

    def qk_local(h, half, b):
        m_scr[b] = scores(h, half, b, 1, kvl)

    def qk_anchor(h, half, b):
        m = scores(h, half, b, 0, kva)
        close(b, m, m_scr[b])

    def pv(h, half, b):
        os = []
        for part, src in ((0, kva), (1, kvl)):
            m = m_scr[b] + penalty if part == 0 else m_scr[b]
            p = jnp.concatenate(
                [jnp.exp2(s_scr[b, :, lo:lo + 128] * LOG2E_SCALE - m).astype(BF16)
                 for lo in range(part * 1024, part * 1024 + 1024, 128)], 1)
            ones = jnp.ones((1024, D), BF16) if part == 0 else onesl[...]
            w = jnp.concatenate([src[1, h].reshape(1024, D), ones], 1)
            os.append(jnp.dot(p, w, preferred_element_type=F32))
        o = os[0] + os[1]
        o = (o[:, :D] / o[:, D:]).astype(BF16)
        for i in range(R // TOK):
            col = pl.multiple_of((h * 8 + half * 4 + i) * D, D)
            out_ref[:, pl.ds(col, D)] = o[i * TOK:(i + 1) * TOK]

    def rotate_queries(h, _):
        for i in range(8):
            col = pl.multiple_of((h * 8 + i) * D, D)
            qs[pl.ds(col, TOK), :] = rotate(q_in[:, pl.ds(col, D)])
        return 0

    pl.semaphore_wait(bar, 15)
    c_p().start()
    l1(0)
    l1(1)

    t_i = lax.broadcasted_iota(jnp.int32, (TOK, 256), 0)
    k_i = lax.broadcasted_iota(jnp.int32, (TOK, 256), 1)
    bias[...] = jnp.where(k_i <= t_i + xl * TOK, 0.0, MASKED).astype(F32)
    onesl[768:1024] = jnp.ones((256, D), BF16)
    cand2[c] = kvl[c, :, 3, xl]
    for d in (1, 2, 3):
        rows = slice((3 - d) * 256, (4 - d) * 256)

        @pl.when(y >= d)
        def _():
            onesl[rows] = jnp.ones((256, D), BF16)

        @pl.when(y < d)
        def _():
            onesl[rows] = jnp.zeros((256, D), BF16)

            def fill(h, _):
                first = kvl[0, h, 3, xl][0:1].astype(F32)
                kvl[0, h, 3 - d] = jnp.broadcast_to(first[None], (2, TOK, D)).astype(BF16)
                kvl[1, h, 3 - d] = jnp.zeros((2, TOK, D), BF16)
                return 0

            lax.fori_loop(0, KV, fill, 0)

    c_p_in().wait_recv()
    chosen[...] = cand2[own_ref[0] % 2]
    for r in range(7):
        c_a0(r).start()
    cand8[h0] = chosen[h0]
    q_load.wait()
    lax.fori_loop(0, 4, rotate_queries, 0)
    l2k(0)
    l2v(0)
    for r in range(7):
        c_a0_in(r).wait_recv()
    kva[c, h0, head] = cand8[own_ref[0] // 2]
    for r in range(7):
        c_a2(r).start()
    lax.fori_loop(4, 8, rotate_queries, 0)
    l2k(1)
    l2v(1)
    l2c(0)
    for r in range(7):
        c_a2_in(r).wait_recv()
    c_cx(0, c).start()
    for n in (1, 2, 3, 6):
        c_a3(n).start()
    l1(2)
    l1(3)
    l3(0)
    first, second = head_of(0), head_of(1)
    qk_local(first, 0, 0)
    qk_local(first, 1, 1)
    cx_in(0)

    qk_anchor(first, 0, 0)
    l2c(1)
    qk_anchor(first, 1, 1)
    pv(first, 0, 0)
    l2k(2)
    l2v(2)
    pv(first, 1, 1)
    qk_local(second, 0, 0)
    a_in(1)
    qk_local(second, 1, 1)
    a_in(2)
    a_in(3)
    l_sent(0)
    c_p().wait_send()
    for r in range(7):
        c_a0(r).wait_send()
        c_a2(r).wait_send()
    cx_in(1)
    qk_anchor(second, 0, 0)
    l2k(3)
    l2c(2)
    l3(1)
    qk_anchor(second, 1, 1)
    pv(second, 0, 0)
    l2v(3)
    cx_in(2)
    qk(head_of(2), 0, 0)
    pv(second, 1, 1)

    POLLS = {
        (1, 0): lambda: (l2c(3),),
        (1, 1): lambda: (l3(2), cx_in(3),),
        (1, 2): lambda: (a_in(4), a_in(5), a_in(6),),
        (1, 3): lambda: (cx_in(4),),
        (2, 1): lambda: (cx_in(5), a_in(7),),
        (2, 2): lambda: (l3(3),),
        (2, 3): lambda: (cx_in(6),),
        (3, 1): lambda: (cx_in(7),),
    }

    def two_heads(it, _):
        def poll(j):
            for (i, jj), f in POLLS.items():
                if jj == j:
                    @pl.when(it == i)
                    def _():
                        f()

        def by_it(values):
            return jnp.where(it == 1, values[0], jnp.where(it == 2, values[1], values[2]))

        ha = by_it([head_of(n) for n in (2, 4, 6)])
        hb = by_it([head_of(n) for n in (3, 5, 7)])
        hn = by_it([head_of(n) for n in (4, 6, 7)])

        poll(0)
        qk(ha, 1, 1)
        pv(ha, 0, 0)
        poll(1)
        qk(hb, 0, 0)
        pv(ha, 1, 1)
        poll(2)
        qk(hb, 1, 1)
        pv(hb, 0, 0)
        poll(3)

        @pl.when(it < 3)
        def _():
            qk(hn, 0, 0)
            pv(hb, 1, 1)

        @pl.when(it == 3)
        def _():
            pv(hb, 1, 1)

        return 0

    lax.fori_loop(1, 4, two_heads, 0)

    for g in range(1, 4):
        l_sent(g)
    for r in range(7):
        c_a3(r + 1).wait_send()
    for n in range(KV):
        c_cx(n, c).wait_send()


def local(query_rows, token_keys, token_values, offsets, anchor_owner):
    exponents = np.arange(D // 2, dtype=np.float32) * np.float32(2.0 / D)
    inverse = (np.float64(ROPE_THETA) ** (-exponents.astype(np.float64))).astype(np.float32)
    inv = jnp.asarray(np.concatenate([inverse, inverse])[None, :])
    hbm = pl.BlockSpec(memory_space=pl.ANY)
    vmem = pl.BlockSpec(memory_space=pltpu.VMEM)
    smem = pl.BlockSpec(memory_space=pltpu.SMEM)
    dma = pltpu.SemaphoreType.DMA
    return pl.pallas_call(
        kernel,
        out_shape=pltpu.VMEM(query_rows.shape, BF16),
        in_specs=[hbm, vmem, vmem, vmem, smem, smem],
        out_specs=vmem,
        scratch_shapes=[
            pltpu.VMEM((TOK, QUERY_HEADS * D), BF16),
            pltpu.VMEM((2, KV, 4, 2, TOK, D), BF16),
            pltpu.VMEM((2, KV, 8, TOK, D), BF16),
            pltpu.VMEM((2, KV, TOK, D), BF16),
            pltpu.VMEM((KV, TOK, D), BF16),
            pltpu.VMEM((KV, TOK, D), BF16),
            pltpu.VMEM((QUERY_HEADS * TOK, D), BF16),
            pltpu.VMEM((2, R, 2048), F32),
            pltpu.VMEM((2, R, D), F32),
            pltpu.VMEM((TOK, 256), F32),
            pltpu.VMEM((1024, D), BF16),
            pltpu.VMEM((TOK, D), F32),
            pltpu.VMEM((TOK, D), F32),
            dma, dma((4,)), dma((4,)), dma((4, 4)), dma((4, 4)), dma((4, 4)), dma((4, 4)),
            dma((4,)), dma((4,)), dma((4,)), dma, dma, dma((8,)), dma((8,)), dma((8,)), dma((8,)),
            dma((8,)), dma((8,)), dma((8,)), dma((8,)),
        ],
        compiler_params=pltpu.CompilerParams(
            collective_id=0, has_side_effects=True, vmem_limit_bytes=60 * 2**20
        ),
        name="star_attention",
    )(query_rows, token_keys, token_values, inv, offsets, anchor_owner)


def solution(mesh):
    return jax.shard_map(
        local,
        mesh=mesh,
        in_specs=(
            P(("hst", "head"), None),
            P(("hst", "head"), None),
            P(("hst", "head"), None),
            P("hst"),
            P(),
        ),
        out_specs=P(("hst", "head"), None),
        check_vma=False,
    )
```
